512 devices in a mesh: layer: 64 (over x, y, z_hi, core), tok: 8 (over z_lo).
Axes of the slice: x: 4, y: 4, z: 16 (z_hi: 2, z_lo: 8; z = z_hi * 8 + z_lo), core: 2. Of those that a mesh axis runs over, the one named last changes fastest.
Arguments:
- residuals: bfloat16 [2, 512, 8192], P(None, None, 'layer'), may hold values from -6 to 6
- w_enc: bfloat16 [2, 8192, 16384], P(None, 'layer', 'tok'), may hold values from -0.0625 to 0.0625
- b_enc: float32 [2, 16384], P(None, 'tok'), may hold values from -3 to 3
- w_dec: bfloat16 [2, 16384, 16384], P(None, 'tok', 'layer'), may hold values from -0.0625 to 0.0625
- b_dec: float32 [16384], P('layer'), may hold values from -3 to 3
- act_slots: int32 [2, 8, 32], replicated, may hold values from -1 to 127, as said below
Outputs:
- recon: bfloat16 [512, 16384], P('tok', 'layer')
The draws below stay inside these ranges and needn't reach their ends.
Inputs may be any that keep to these rules, and one draw needn't show every extreme that they name: `act_slots`: entry k of a list names a block among the 16 blocks numbered from (k // 4) * 16, or is -1 for an empty slot. In each group of 4 slots the live entries come first and at least one is live; blocks within a list are distinct; in every list some group is full.
All inputs are finite; a program needn't handle non-finite values.
Results may differ from the reference program's by a relative error of at most 0.0043.
Values may be sent and summed in bfloat16 or wider, within the bound.
A program may use at most 64 MiB of HBM per device.

```python
import jax
import jax.numpy as jnp
from jax import lax

D = 8192
FB_DEV = 16
CAP = 4
SRC = 2
TGT = 2
TB = 64
TOKENS = 512
FW = 16384
NB_SLOTS = 32
NTB = 8


def draw_act_slots(key, part):
    key = jax.random.fold_in(key, 17)
    groups = NB_SLOTS // CAP
    key_count, key_full, key_pick = jax.random.split(key, 3)
    counts = jax.random.randint(key_count, (SRC, NTB, groups), 1, CAP + 1)
    full_group = jax.random.randint(key_full, (SRC, NTB, 1), 0, groups)
    counts = jnp.where(jnp.arange(groups)[None, None, :] == full_group, CAP, counts)
    scores = jax.random.randint(key_pick, (SRC, NTB, groups, FB_DEV), 0, 1048576) * FB_DEV + jnp.arange(FB_DEV)
    picked = jnp.argsort(scores, axis=-1)[..., :CAP]
    blocks = picked + jnp.arange(groups)[None, None, :, None] * FB_DEV
    is_used = jnp.arange(CAP)[None, None, None, :] < counts[..., None]
    return jnp.where(is_used, blocks, -1).reshape(SRC, NTB, groups * CAP).astype(jnp.int32)


def block_levels(stream_key, extent, cuts, least, top_value):
    loudness = 1.0
    for dim, shards_of in cuts:
        draws = jax.random.uniform(jax.random.fold_in(jax.random.fold_in(stream_key, 6), dim), (shards_of,), jnp.float32, least / len(cuts), top_value / len(cuts))
        loudness = loudness * jnp.repeat(jnp.exp(draws), extent[dim] // shards_of).reshape((-1,) + (1,) * (len(extent) - 1 - dim))
    return loudness


def scatter_about(rng, shape, width, limit, cuts=(), kind=jnp.bfloat16):
    entries = jax.random.normal(rng, shape, jnp.float32) * width
    if len(cuts) > 0:
        entries = block_levels(rng, shape, cuts, -0.22, 0.18) * entries
    return jnp.clip(entries, min=-limit, max=limit).astype(kind)


def setup_inputs(seed: int = 0) -> dict:
    splits = jax.random.split(jax.random.key(seed), 7)
    residuals = scatter_about(splits[0], (SRC, TOKENS, D), 1.0, 6.0, ((2, 64),))
    w_enc = scatter_about(splits[1], (SRC, D, FW), D ** -0.5, 0.0625, ((1, 64), (2, 8)))
    b_enc = scatter_about(splits[2], (SRC, FW), 0.5, 3.0, ((1, 8),), jnp.float32)
    w_dec = scatter_about(splits[3], (SRC, FW, TGT * D), (SRC * FW // 4) ** -0.5, 0.0625, ((1, 8), (2, 64)))
    b_dec = scatter_about(splits[4], (TGT * D,), 0.5, 3.0, ((0, 64),), jnp.float32)
    act_slots = draw_act_slots(jax.random.fold_in(splits[6], 71), 0)
    return {"residuals": residuals, "w_enc": w_enc, "b_enc": b_enc, "w_dec": w_dec, "b_dec": b_dec, "act_slots": act_slots}


def reference(residuals, w_enc, b_enc, w_dec, b_dec, act_slots):
    offsets = jnp.arange(128, dtype=jnp.int32)

    def one_block(operand):
        rows_x, slot_row = operand
        summed = jnp.zeros((TB, TGT * D), jnp.float32)
        for source in range(SRC):
            is_live = slot_row[source] >= 0
            block_ids = jnp.where(is_live, slot_row[source], 0).astype(jnp.int32)
            columns = (block_ids[:, None] * 128 + offsets[None, :]).reshape(-1).astype(jnp.int32)
            keep_mask = jnp.repeat(is_live.astype(jnp.float32), 128)
            chosen = jnp.take(w_enc[source], columns, axis=1)
            pre_part = jnp.dot(rows_x[source], chosen, preferred_element_type=jnp.float32)
            pre_part = pre_part + jnp.take(b_enc[source], columns).astype(jnp.float32)
            features = (jnp.maximum(pre_part, 0.0) * keep_mask).astype(jnp.bfloat16)
            decoder = jnp.take(w_dec[source], columns, axis=0)
            summed = summed + jnp.dot(features, decoder, preferred_element_type=jnp.float32)
        return (summed + b_dec.astype(jnp.float32)).astype(jnp.bfloat16)

    blocked = residuals.reshape(SRC, NTB, TB, D).transpose(1, 0, 2, 3)
    slot_lists = act_slots.transpose(1, 0, 2)
    result = lax.map(one_block, (blocked, slot_lists))
    return result.reshape(TOKENS, TGT * D)
```

```python
import functools

import jax
import jax.numpy as jnp
from jax import lax
from jax.experimental import pallas as pl
from jax.experimental.pallas import tpu as pltpu
from jax.sharding import PartitionSpec as P

MESH = pl.DeviceIdType.MESH
CHUNKS = 2
F32 = jnp.float32
BF16 = jnp.bfloat16


def device(x, y, zh, c, t):
    return (((x * 4 + y) * 2 + zh) * 2 + c, t)


def kernel(
    slots_ref, x_hbm, we_hbm, be_hbm, wd_hbm, out_ref,
    xfull, wfull, be, wd, pbuf, rs_land, zh_send, zh_land, fown, feat, zbuf, zland,
    local_sem, in_send, in_recv, wd_send, wd_recv, rs_send, rs_recv, zh_ss, zh_rs,
    ag_send, own_send, ag_recv, zl_send, zl_recv,
):
    layer = lax.axis_index("layer")
    t = lax.axis_index("tok")
    c = lax.rem(layer, 2)
    zh = lax.rem(layer // 2, 2)
    y = lax.rem(layer // 4, 4)
    x = layer // 16
    p = x * 4 + y
    half = lax.rem(p // 4, 2)
    pair = p // 8
    partner = device(x, y, zh, 1 - c, t)
    opposite = device(x, y, 1 - zh, c, t)

    def plane(d):
        return lax.rem(x + d // 4, 4), lax.rem(y + lax.rem(d, 4), 4)

    barrier = pltpu.get_barrier_semaphore()

    def signal(dev):
        pl.semaphore_signal(barrier, inc=1, device_id=dev, device_id_type=MESH)

    signal(partner)
    signal(opposite)

    def greet_plane(d, carry):
        px, py = plane(d)
        signal(device(px, py, zh, 0, t))
        signal(device(px, py, zh, 1, t))
        return carry

    def greet_line(d, carry):
        pt = lax.rem(t + d, 8)
        signal(device(x, y, zh, 0, pt))
        signal(device(x, y, zh, 1, pt))
        return carry

    lax.fori_loop(1, 16, greet_plane, 0)
    lax.fori_loop(1, 8, greet_line, 0)

    local = [
        pltpu.make_async_copy(x_hbm.at[c], xfull.at[:, pl.ds(0, 128)], local_sem.at[1]),
        pltpu.make_async_copy(wd_hbm, wd.at[0], local_sem.at[3]),
    ]
    for i in range(16):
        part = pl.ds(i * 128, 128)
        pltpu.make_async_copy(we_hbm.at[c, :, part], wfull.at[i, pl.ds(0, 128)], local_sem.at[0]).start()
    for copy in local:
        copy.start()
    for i in range(16):
        pltpu.make_async_copy(be_hbm.at[:, pl.ds(i * 128, 128)], be.at[i], local_sem.at[2]).start()

    pl.semaphore_wait(barrier, 2 + 30 + 14)

    def remote(src, dst, send, recv, dev):
        return pltpu.make_async_remote_copy(
            src_ref=src, dst_ref=dst, send_sem=send, recv_sem=recv, device_id=dev, device_id_type=MESH
        )

    swap_w = [
        remote(
            we_hbm.at[1 - c, :, pl.ds(i * 128, 128)], wfull.at[i, pl.ds(128, 128)],
            in_send.at[0], in_recv.at[0], partner,
        )
        for i in range(16)
    ]
    half_w = wfull.at[:, pl.ds(128, 128)]
    swap_x = remote(x_hbm.at[1 - c], xfull.at[:, pl.ds(128, 128)], in_send.at[1], in_recv.at[1], partner)
    swap_d = remote(wd_hbm, wd.at[1], wd_send, wd_recv, partner)
    for copy in swap_w:
        copy.start()
    swap_x.start()
    pltpu.make_async_copy(half_w, half_w, local_sem.at[0]).wait()
    local[0].wait()
    pltpu.make_async_copy(half_w, half_w, in_recv.at[0]).wait()
    swap_x.wait_recv()
    swap_d.start()

    def block_id(source, b, s):
        slot = slots_ref[source, b, 4 * t + s]
        return jnp.maximum(slot - 16 * t, 0), jnp.minimum(slot + 1, 1)

    for k in range(CHUNKS):
        for j in range(4):
            b = 4 * k + j
            cols = [wfull[block_id(c, b, s)[0]] for s in range(4)]
            w = jnp.concatenate(cols, axis=1)
            part = jnp.dot(xfull[pl.ds(b * 64, 64), :], w, preferred_element_type=F32)
            pbuf[k, pl.ds(j * 64, 64), :] = part.astype(BF16)

        def send_part(d, carry, k=k):
            px, py = plane(d)
            q = px * 4 + py
            remote(
                pbuf.at[k, pl.ds(pl.multiple_of(q * 16, 16), 16)], rs_land.at[k, d - 1],
                rs_send.at[k], rs_recv.at[k], device(px, py, zh, c, t),
            ).start()
            return carry

        lax.fori_loop(1, 16, send_part, 0)

    sums = []
    for k in range(CHUNKS):
        pltpu.make_async_copy(rs_land.at[k], rs_land.at[k], rs_recv.at[k]).wait()
        total = pbuf[k, pl.ds(pl.multiple_of(p * 16, 16), 16), :].astype(F32)
        for d in range(15):
            total = total + rs_land[k, d].astype(F32)
        sums.append(total)
        zh_send[k] = total.astype(BF16)
        remote(zh_send.at[k], zh_land.at[k], zh_ss.at[k], zh_rs.at[k], opposite).start()

    pltpu.make_async_copy(be, be, local_sem.at[2]).wait()
    rows = pl.ds(pl.multiple_of(lax.rem(p, 4) * 16, 16), 16)
    for k in range(CHUNKS):
        b = 4 * k + p // 4
        biases, masks = [], []
        for s in range(4):
            i, live = block_id(c, b, s)
            both = be[i]
            biases.append(jnp.where(c == 0, both[0:1], both[1:2]))
            masks.append(jnp.full((1, 128), live.astype(F32)))
        bias = jnp.concatenate(biases, axis=1)
        mask = jnp.concatenate(masks, axis=1)
        remote(zh_send.at[k], zh_land.at[k], zh_ss.at[k], zh_rs.at[k], opposite).wait_recv()
        pre = sums[k] + zh_land[k].astype(F32) + bias
        fown[k] = (jnp.maximum(pre, 0.0) * mask).astype(BF16)
        mine = feat.at[k, pair, c, rows]

        def send_features(d, carry, k=k, mine=mine):
            px, py = plane(d)
            remote(fown.at[k], mine, ag_send.at[k], ag_recv.at[k, pair], device(px, py, zh, half, t)).start()
            return carry

        @pl.when(c == half)
        def _(k=k, mine=mine):
            pltpu.make_async_copy(fown.at[k], mine, ag_recv.at[k, pair]).start()

        @pl.when(c != half)
        def _(k=k, mine=mine):
            remote(fown.at[k], mine, own_send.at[k], ag_recv.at[k, pair], partner).start()

        lax.fori_loop(1, 16, send_features, 0)

    local[1].wait()
    swap_d.wait_recv()
    for k in range(CHUNKS):
        for j in range(2):
            m = 2 * k + j
            b = 2 * m + c
            pltpu.make_async_copy(feat.at[k, j], feat.at[k, j], ag_recv.at[k, j]).wait()
            ids = [[block_id(s, b, i)[0] for i in range(4)] for s in range(2)]
            f = jnp.concatenate([feat[k, j, 0], feat[k, j, 1]], axis=1)
            for side in range(2):
                w = jnp.concatenate(
                    [
                        wd[side, s, ids[s][i]]
                        for s in range(2)
                        for i in range(4)
                    ],
                    axis=0,
                )
                zbuf[m, side] = jnp.dot(f, w, preferred_element_type=F32).astype(BF16)

            for side in range(2):
                core = c if side == 0 else 1 - c
                whole = remote(
                    zbuf.at[m, side], zland.at[t], zl_send.at[m, side], zl_recv, device(x, y, zh, core, b)
                )
                if side == 0:

                    @pl.when(b == t)
                    def _(m=m):
                        pltpu.make_async_copy(zbuf.at[m, 0], zland.at[t], zl_recv).start()

                    @pl.when(b != t)
                    def _(whole=whole):
                        whole.start()
                else:
                    whole.start()

    pltpu.make_async_copy(zland, zland, zl_recv).wait()
    result = zland[0].astype(F32)
    for i in range(1, 8):
        result = result + zland[i].astype(F32)
    out_ref[...] = result

    pltpu.make_async_copy(half_w, half_w, in_send.at[0]).wait()
    swap_x.wait_send()
    swap_d.wait_send()
    for k in range(CHUNKS):
        pltpu.make_async_copy(rs_land.at[k], rs_land.at[k], rs_send.at[k]).wait()
        pltpu.make_async_copy(rs_land.at[k], rs_land.at[k], ag_send.at[k]).wait()
        remote(zh_send.at[k], zh_land.at[k], zh_ss.at[k], zh_rs.at[k], opposite).wait_send()

        @pl.when(c != half)
        def _(k=k):
            remote(fown.at[k], fown.at[k], own_send.at[k], ag_recv.at[k, pair], partner).wait_send()

    for m in range(4):
        b = 2 * m + c

        @pl.when(b != t)
        def _(m=m):
            remote(zbuf.at[m, 0], zland.at[t], zl_send.at[m, 0], zl_recv, partner).wait_send()

        remote(zbuf.at[m, 1], zland.at[t], zl_send.at[m, 1], zl_recv, partner).wait_send()


def per_device(residuals, w_enc, b_enc, w_dec, b_dec, act_slots):
    dma = pltpu.SemaphoreType.DMA
    summed = pl.pallas_call(
        kernel,
        out_shape=jax.ShapeDtypeStruct((64, 256), F32),
        in_specs=[pl.BlockSpec(memory_space=pltpu.SMEM)] + [pl.BlockSpec(memory_space=pl.ANY)] * 4,
        out_specs=pl.BlockSpec(memory_space=pltpu.VMEM),
        scratch_shapes=[
            pltpu.VMEM((512, 256), BF16),
            pltpu.VMEM((16, 256, 128), BF16),
            pltpu.VMEM((16, 2, 128), F32),
            pltpu.VMEM((2, 2, 16, 128, 256), BF16),
            pltpu.VMEM((CHUNKS, 256, 512), BF16),
            pltpu.VMEM((CHUNKS, 15, 16, 512), BF16),
            pltpu.VMEM((CHUNKS, 16, 512), BF16),
            pltpu.VMEM((CHUNKS, 16, 512), BF16),
            pltpu.VMEM((CHUNKS, 16, 512), BF16),
            pltpu.VMEM((CHUNKS, 2, 2, 64, 512), BF16),
            pltpu.VMEM((4, 2, 64, 256), BF16),
            pltpu.VMEM((8, 64, 256), BF16),
            dma((4,)),
            dma((2,)),
            dma((2,)),
            dma,
            dma,
            dma((CHUNKS,)),
            dma((CHUNKS,)),
            dma((CHUNKS,)),
            dma((CHUNKS,)),
            dma((CHUNKS,)),
            dma((CHUNKS,)),
            dma((CHUNKS, 2)),
            dma((4, 2)),
            dma,
        ],
        compiler_params=pltpu.CompilerParams(
            collective_id=0, has_side_effects=True, vmem_limit_bytes=60 * 2**20
        ),
        cost_estimate=pl.CostEstimate(flops=402653184, bytes_accessed=4194304, transcendentals=0),
    )(act_slots, residuals, w_enc, b_enc, w_dec.reshape(2, 16, 128, 256))
    return (summed + b_dec[None, :]).astype(BF16)


def solution(mesh):
    in_specs = (
        P(None, None, "layer"),
        P(None, "layer", "tok"),
        P(None, "tok"),
        P(None, "tok", "layer"),
        P("layer"),
        P(),
    )
    return jax.shard_map(
        per_device, mesh=mesh, in_specs=in_specs, out_specs=P("tok", "layer"), check_vma=False
    )
```

```python
import functools

import jax
import jax.numpy as jnp
from jax import lax
from jax.experimental import pallas as pl
from jax.experimental.pallas import tpu as pltpu
from jax.sharding import PartitionSpec as P

MESH = pl.DeviceIdType.MESH
CHUNKS = 2
F32 = jnp.float32
BF16 = jnp.bfloat16


def device(x, y, zh, c, t):
    return (((x * 4 + y) * 2 + zh) * 2 + c, t)


def kernel(
    slots_ref, x_hbm, we_hbm, be_hbm, wd_hbm, bd_ref, out_ref,
    xv, we, be, wd, keep, give, take, pbuf, rs_land, zh_send, zh_land, fown, feat, zbuf, zland,
    local_sem, give_send, give_recv, wd_send, wd_recv, rs_send, rs_recv, zh_ready, zh_ss, zh_rs,
    ag_send, own_send, ag_recv, zl_send, zl_recv,
):
    layer = lax.axis_index("layer")
    t = lax.axis_index("tok")
    c = lax.rem(layer, 2)
    zh = lax.rem(layer // 2, 2)
    y = lax.rem(layer // 4, 4)
    x = layer // 16
    p = x * 4 + y
    half = lax.rem(x, 2)
    pair = x // 2
    crossed = lax.rem(half + c, 2)
    partner = device(x, y, zh, 1 - c, t)
    opposite = device(x, y, 1 - zh, c, t)

    def plane(d):
        return lax.rem(x + d // 4, 4), lax.rem(y + lax.rem(d, 4), 4)

    barrier = pltpu.get_barrier_semaphore()

    def signal(dev):
        pl.semaphore_signal(barrier, inc=1, device_id=dev, device_id_type=MESH)

    def greet_same(d, carry):
        px, py = plane(d)
        signal(device(px, py, zh, c, t))
        return carry

    def greet_other(d, carry):
        px, py = c + 2 * (d // 4), lax.rem(d, 4)

        @pl.when((px != x) | (py != y))
        def _():
            signal(device(px, py, zh, 1 - c, t))

        return carry

    def greet_line(d, carry):
        signal(device(x, y, zh, lax.rem(t, 2), lax.rem(t + d, 8)))
        return carry

    lax.fori_loop(1, 16, greet_same, 0)
    lax.fori_loop(0, 8, greet_other, 0)
    signal(partner)
    lax.fori_loop(1, 8, greet_line, 0)

    @pl.when(zh == 0)
    def _():
        signal(opposite)

    load_x = pltpu.make_async_copy(x_hbm, xv, local_sem.at[0])
    load_d = pltpu.make_async_copy(wd_hbm, wd.at[0], local_sem.at[3])
    load_x.start()
    for s in range(2):
        for i in range(16):
            cut = pl.ds(i * 128, 128)
            pltpu.make_async_copy(we_hbm.at[s, :, cut], we.at[s, i], local_sem.at[1]).start()
    load_d.start()
    for i in range(16):
        pltpu.make_async_copy(be_hbm.at[:, pl.ds(i * 128, 128)], be.at[i], local_sem.at[2]).start()
    load_x.wait()
    pltpu.make_async_copy(we, we, local_sem.at[1]).wait()

    def remote(src, dst, send, recv, dev):
        return pltpu.make_async_remote_copy(
            src_ref=src, dst_ref=dst, send_sem=send, recv_sem=recv, device_id=dev, device_id_type=MESH
        )

    def block_id(source, b, s):
        slot = slots_ref[source, b, 4 * t + s]
        return jnp.maximum(slot - 16 * t, 0), jnp.minimum(slot + 1, 1)

    for target, source in ((keep, c), (give, 1 - c)):
        for b in range(8):
            w = jnp.concatenate([we[source, block_id(source, b, s)[0]] for s in range(4)], axis=1)
            target[b] = jnp.dot(xv[source, pl.ds(b * 64, 64), :], w, preferred_element_type=F32)

    pl.semaphore_wait(barrier, 15 + 15 * crossed + 1 + 6 + 2 * lax.rem(t + c, 2) + zh)

    @pl.when(zh == 1)
    def _():
        pl.semaphore_signal(zh_ready, inc=1, device_id=opposite, device_id_type=MESH)

    gives = []
    for k in range(CHUNKS):
        for i in range(4):
            n = 4 * k + lax.rem(x + i, 4)
            gives.append(remote(give.at[n], take.at[n], give_send.at[k, i], give_recv.at[k, i], partner))
            gives[-1].start()
    for k in range(CHUNKS):
        for i in range(4):
            px = lax.rem(x + i, 4)
            n = 4 * k + px
            gives[4 * k + i].wait_recv()
            pbuf[n] = (keep[n] + take[n]).astype(BF16)

            def send_part(j, carry, k=k, i=i, px=px, n=n):
                py = lax.rem(y + j, 4)
                remote(
                    pbuf.at[n, pl.ds(pl.multiple_of(py * 16, 16), 16)], rs_land.at[k, 4 * i + j - 1],
                    rs_send.at[k], rs_recv.at[k], device(px, py, zh, c, t),
                ).start()
                return carry

            lax.fori_loop(1 if i == 0 else 0, 4, send_part, 0)

    swap_d = remote(wd_hbm, wd.at[1], wd_send, wd_recv, partner)
    swap_d.start()

    @pl.when(zh == 0)
    def _():
        pl.semaphore_wait(zh_ready, 1)

    rows = pl.ds(pl.multiple_of(y * 16, 16), 16)
    sums = []
    for k in range(CHUNKS):
        pltpu.make_async_copy(rs_land.at[k], rs_land.at[k], rs_recv.at[k]).wait()
        total = pbuf[4 * k + x, rows, :].astype(F32)
        for d in range(15):
            total = total + rs_land[k, d].astype(F32)
        sums.append(total)
        zh_send[k] = total.astype(BF16)
        remote(zh_send.at[k], zh_land.at[k], zh_ss.at[k], zh_rs.at[k], opposite).start()

    pltpu.make_async_copy(be, be, local_sem.at[2]).wait()
    for k in range(CHUNKS):
        b = 4 * k + x
        biases, masks = [], []
        for s in range(4):
            i, live = block_id(c, b, s)
            both = be[i]
            biases.append(jnp.where(c == 0, both[0:1], both[1:2]))
            masks.append(jnp.full((1, 128), live.astype(F32)))
        bias = jnp.concatenate(biases, axis=1)
        mask = jnp.concatenate(masks, axis=1)
        remote(zh_send.at[k], zh_land.at[k], zh_ss.at[k], zh_rs.at[k], opposite).wait_recv()
        pre = sums[k] + zh_land[k].astype(F32) + bias
        fown[k] = (jnp.maximum(pre, 0.0) * mask).astype(BF16)
        mine = feat.at[k, pair, c, rows]

        def send_features(d, carry, k=k, mine=mine):
            px, py = plane(d)
            remote(fown.at[k], mine, ag_send.at[k], ag_recv.at[k, pair], device(px, py, zh, half, t)).start()
            return carry

        lax.fori_loop(1, 16, send_features, 0)

        @pl.when(c == half)
        def _(k=k, mine=mine):
            pltpu.make_async_copy(fown.at[k], mine, ag_recv.at[k, pair]).start()

        @pl.when(c != half)
        def _(k=k, mine=mine):
            remote(fown.at[k], mine, own_send.at[k], ag_recv.at[k, pair], partner).start()

    load_d.wait()
    swap_d.wait_recv()
    for k in range(CHUNKS):
        for j in range(2):
            m = 2 * k + j
            b = 2 * m + c
            pltpu.make_async_copy(feat.at[k, j], feat.at[k, j], ag_recv.at[k, j]).wait()
            ids = [[block_id(s, b, i)[0] for i in range(4)] for s in range(2)]
            f = jnp.concatenate([feat[k, j, 0], feat[k, j, 1]], axis=1)

            for side in range(2):
                w = jnp.concatenate([wd[side, s, ids[s][i]] for s in range(2) for i in range(4)], axis=0)
                zbuf[m, side] = jnp.dot(f, w, preferred_element_type=F32).astype(BF16)
                core = c if side == 0 else 1 - c
                whole = remote(
                    zbuf.at[m, side], zland.at[t], zl_send.at[m, side], zl_recv, device(x, y, zh, core, b)
                )
                if side == 0:

                    @pl.when(b == t)
                    def _(m=m):
                        pltpu.make_async_copy(zbuf.at[m, 0], zland.at[t], zl_recv).start()

                    @pl.when(b != t)
                    def _(whole=whole):
                        whole.start()
                else:
                    whole.start()

    pltpu.make_async_copy(zland, zland, zl_recv).wait()
    result = zland[0].astype(F32)
    for i in range(1, 8):
        result = result + zland[i].astype(F32)
    out_ref[...] = (result + bd_ref[...]).astype(BF16)

    swap_d.wait_send()
    for copy in gives:
        copy.wait_send()
    for k in range(CHUNKS):
        pltpu.make_async_copy(rs_land.at[k], rs_land.at[k], rs_send.at[k]).wait()
        pltpu.make_async_copy(rs_land.at[k], rs_land.at[k], ag_send.at[k]).wait()
        remote(zh_send.at[k], zh_land.at[k], zh_ss.at[k], zh_rs.at[k], opposite).wait_send()

        @pl.when(c != half)
        def _(k=k):
            remote(fown.at[k], fown.at[k], own_send.at[k], ag_recv.at[k, pair], partner).wait_send()

    for m in range(4):
        b = 2 * m + c

        @pl.when(b != t)
        def _(m=m):
            remote(zbuf.at[m, 0], zland.at[t], zl_send.at[m, 0], zl_recv, partner).wait_send()

        remote(zbuf.at[m, 1], zland.at[t], zl_send.at[m, 1], zl_recv, partner).wait_send()


def per_device(residuals, w_enc, b_enc, w_dec, b_dec, act_slots):
    dma = pltpu.SemaphoreType.DMA
    return pl.pallas_call(
        kernel,
        out_shape=jax.ShapeDtypeStruct((64, 256), BF16),
        in_specs=[pl.BlockSpec(memory_space=pltpu.SMEM)]
        + [pl.BlockSpec(memory_space=pl.ANY)] * 4
        + [pl.BlockSpec(memory_space=pltpu.VMEM)],
        out_specs=pl.BlockSpec(memory_space=pltpu.VMEM),
        scratch_shapes=[
            pltpu.VMEM((2, 512, 128), BF16),
            pltpu.VMEM((2, 16, 128, 128), BF16),
            pltpu.VMEM((16, 2, 128), F32),
            pltpu.VMEM((2, 2, 16, 128, 256), BF16),
            pltpu.VMEM((8, 64, 512), F32),
            pltpu.VMEM((8, 64, 512), F32),
            pltpu.VMEM((8, 64, 512), F32),
            pltpu.VMEM((8, 64, 512), BF16),
            pltpu.VMEM((CHUNKS, 15, 16, 512), BF16),
            pltpu.VMEM((CHUNKS, 16, 512), BF16),
            pltpu.VMEM((CHUNKS, 16, 512), BF16),
            pltpu.VMEM((CHUNKS, 16, 512), BF16),
            pltpu.VMEM((CHUNKS, 2, 2, 64, 512), BF16),
            pltpu.VMEM((4, 2, 64, 256), BF16),
            pltpu.VMEM((8, 64, 256), BF16),
            dma((4,)),
            dma((CHUNKS, 4)),
            dma((CHUNKS, 4)),
            dma,
            dma,
            dma((CHUNKS,)),
            dma((CHUNKS,)),
            pltpu.SemaphoreType.REGULAR,
            dma((CHUNKS,)),
            dma((CHUNKS,)),
            dma((CHUNKS,)),
            dma((CHUNKS,)),
            dma((CHUNKS, 2)),
            dma((4, 2)),
            dma,
        ],
        compiler_params=pltpu.CompilerParams(
            collective_id=0, has_side_effects=True, vmem_limit_bytes=60 * 2**20
        ),
        cost_estimate=pl.CostEstimate(flops=402653184, bytes_accessed=4194304, transcendentals=0),
    )(act_slots, residuals, w_enc, b_enc, w_dec.reshape(2, 16, 128, 256), b_dec.reshape(1, 256))


def solution(mesh):
    in_specs = (
        P(None, None, "layer"),
        P(None, "layer", "tok"),
        P(None, "tok"),
        P(None, "tok", "layer"),
        P("layer"),
        P(),
    )
    return jax.shard_map(
        per_device, mesh=mesh, in_specs=in_specs, out_specs=P("tok", "layer"), check_vma=False
    )
```

```python
import functools

import jax
import jax.numpy as jnp
from jax import lax
from jax.experimental import pallas as pl
from jax.experimental.pallas import tpu as pltpu
from jax.sharding import PartitionSpec as P

MESH = pl.DeviceIdType.MESH
CHUNKS = 2
F32 = jnp.float32
BF16 = jnp.bfloat16
FAR_FIRST = (10, 6, 9, 11, 14, 2, 5, 7, 8, 13, 15, 1, 3, 4, 12)


def device(x, y, zh, c, t):
    return (((x * 4 + y) * 2 + zh) * 2 + c, t)


def kernel(
    slots_ref, x_hbm, we_hbm, be_hbm, wd_hbm, bd_ref, out_ref,
    xv, we, be, wd, keep, give, take, pbuf, rs_land, zh_send, zh_land, fown, feat, zbuf, zland,
    local_sem, give_send, give_recv, wd_send, wd_recv, rs_send, rs_recv, zh_ready, zh_ss, zh_rs,
    ag_send, own_send, ag_recv, zl_send, zl_recv,
):
    layer = lax.axis_index("layer")
    t = lax.axis_index("tok")
    c = lax.rem(layer, 2)
    zh = lax.rem(layer // 2, 2)
    y = lax.rem(layer // 4, 4)
    x = layer // 16
    half = x // 2
    pair = lax.rem(x, 2)
    crossed = lax.rem(half + c, 2)
    partner = device(x, y, zh, 1 - c, t)
    opposite = device(x, y, 1 - zh, c, t)

    def plane(d):
        return lax.rem(x + d // 4, 4), lax.rem(y + lax.rem(d, 4), 4)

    barrier = pltpu.get_barrier_semaphore()

    def signal(dev):
        pl.semaphore_signal(barrier, inc=1, device_id=dev, device_id_type=MESH)

    def greet_other(d, carry):
        px, py = 2 * c + d // 4, lax.rem(d, 4)

        @pl.when((px != x) | (py != y))
        def _():
            signal(device(px, py, zh, 1 - c, t))

        return carry

    def greet_line(d, carry):
        signal(device(x, y, zh, t // 4, lax.rem(t + d, 8)))
        return carry

    for d in FAR_FIRST:
        px, py = plane(d)
        signal(device(px, py, zh, c, t))
    lax.fori_loop(0, 8, greet_other, 0)
    signal(partner)
    lax.fori_loop(1, 8, greet_line, 0)

    @pl.when(zh == 0)
    def _():
        signal(opposite)

    load_x = pltpu.make_async_copy(x_hbm, xv, local_sem.at[0])
    load_d = pltpu.make_async_copy(wd_hbm, wd.at[0], local_sem.at[3])
    load_x.start()
    for s in range(2):
        for i in range(16):
            cut = pl.ds(i * 128, 128)
            pltpu.make_async_copy(we_hbm.at[s, :, cut], we.at[s, i], local_sem.at[1]).start()
    load_d.start()
    for i in range(16):
        pltpu.make_async_copy(be_hbm.at[:, pl.ds(i * 128, 128)], be.at[i], local_sem.at[2]).start()
    load_x.wait()
    pltpu.make_async_copy(we, we, local_sem.at[1]).wait()

    def remote(src, dst, send, recv, dev):
        return pltpu.make_async_remote_copy(
            src_ref=src, dst_ref=dst, send_sem=send, recv_sem=recv, device_id=dev, device_id_type=MESH
        )

    def block_id(source, b, s):
        slot = slots_ref[source, b, 4 * t + s]
        return jnp.maximum(slot - 16 * t, 0), jnp.minimum(slot + 1, 1)

    for target, source in ((keep, c), (give, 1 - c)):
        for b in range(8):
            w = jnp.concatenate([we[source, block_id(source, b, s)[0]] for s in range(4)], axis=1)
            target[b] = jnp.dot(xv[source, pl.ds(b * 64, 64), :], w, preferred_element_type=F32)

    pl.semaphore_wait(barrier, 15 + 15 * crossed + 1 + 6 + 2 * lax.rem(t // 4 + c, 2) + zh)

    @pl.when(zh == 1)
    def _():
        pl.semaphore_signal(zh_ready, inc=1, device_id=opposite, device_id_type=MESH)

    gives = []
    order = []
    for m in range(4):
        for i in range(2):
            side = half if i == 0 else 1 - half
            n = m + side * (7 - 2 * m)
            order.append((m, i, side, n))
            gives.append(
                remote(give.at[n], take.at[n], give_send.at[m, i], give_recv.at[m, i], partner)
            )
            gives[-1].start()
    def send_block(m, i, side, n, copy):
        k, px = m // 2, 2 * side + m % 2
        dx = lax.rem(px - x + 4, 4)
        copy.wait_recv()
        pbuf[n] = (keep[n] + take[n]).astype(BF16)

        def send_part(j, carry, k=k, px=px, dx=dx, n=n):
            py = lax.rem(y + j, 4)
            remote(
                pbuf.at[n, pl.ds(pl.multiple_of(py * 16, 16), 16)], rs_land.at[k, 4 * dx + j - 1],
                rs_send.at[k], rs_recv.at[k], device(px, py, zh, c, t),
            ).start()
            return carry

        lax.fori_loop(1, 4, send_part, 0)
        if i == 0:

            @pl.when(px != x)
            def _(send_part=send_part):
                send_part(0, 0)
        else:
            send_part(0, 0)

    first = 4
    for o, copy in zip(order[:first], gives[:first]):
        send_block(*o, copy)

    swap_d = remote(wd_hbm, wd.at[1], wd_send, wd_recv, partner)

    @pl.when(zh == 0)
    def _():
        pl.semaphore_wait(zh_ready, 1)

    rows = pl.ds(pl.multiple_of(y * 16, 16), 16)
    sums = []
    for k in range(CHUNKS):
        pltpu.make_async_copy(rs_land.at[k], rs_land.at[k], rs_recv.at[k]).wait()
        m = 2 * k + pair
        total = pbuf[m + half * (7 - 2 * m), rows, :].astype(F32)
        for d in range(15):
            total = total + rs_land[k, d].astype(F32)
        sums.append(total)
        zh_send[k] = total.astype(BF16)
        remote(zh_send.at[k], zh_land.at[k], zh_ss.at[k], zh_rs.at[k], opposite).start()
        if k == 0:
            for o, copy in zip(order[first:], gives[first:]):
                send_block(*o, copy)

    swap_d.start()

    pltpu.make_async_copy(be, be, local_sem.at[2]).wait()
    for k in range(CHUNKS):
        m = 2 * k + pair
        b = m + half * (7 - 2 * m)
        biases, masks = [], []
        for s in range(4):
            i, live = block_id(c, b, s)
            both = be[i]
            biases.append(jnp.where(c == 0, both[0:1], both[1:2]))
            masks.append(jnp.full((1, 128), live.astype(F32)))
        bias = jnp.concatenate(biases, axis=1)
        mask = jnp.concatenate(masks, axis=1)
        remote(zh_send.at[k], zh_land.at[k], zh_ss.at[k], zh_rs.at[k], opposite).wait_recv()
        pre = sums[k] + zh_land[k].astype(F32) + bias
        fown[k] = (jnp.maximum(pre, 0.0) * mask).astype(BF16)
        mine = feat.at[k, pair, c, rows]

        for d in FAR_FIRST:
            px, py = plane(d)
            remote(fown.at[k], mine, ag_send.at[k], ag_recv.at[k, pair], device(px, py, zh, half, t)).start()

        @pl.when(c == half)
        def _(k=k, mine=mine):
            pltpu.make_async_copy(fown.at[k], mine, ag_recv.at[k, pair]).start()

        @pl.when(c != half)
        def _(k=k, mine=mine):
            remote(fown.at[k], mine, own_send.at[k], ag_recv.at[k, pair], partner).start()

    load_d.wait()
    swap_d.wait_recv()
    for k in range(CHUNKS):
        for j in range(2):
            m = 2 * k + j
            b = m + c * (7 - 2 * m)
            pltpu.make_async_copy(feat.at[k, j], feat.at[k, j], ag_recv.at[k, j]).wait()
            ids = [[block_id(s, b, i)[0] for i in range(4)] for s in range(2)]
            f = jnp.concatenate([feat[k, j, 0], feat[k, j, 1]], axis=1)

            for side in range(2):
                w = jnp.concatenate([wd[side, s, ids[s][i]] for s in range(2) for i in range(4)], axis=0)
                zbuf[m, side] = jnp.dot(f, w, preferred_element_type=F32).astype(BF16)
                core = c if side == 0 else 1 - c
                whole = remote(
                    zbuf.at[m, side], zland.at[t], zl_send.at[m, side], zl_recv, device(x, y, zh, core, b)
                )
                if side == 0:

                    @pl.when(b == t)
                    def _(m=m):
                        pltpu.make_async_copy(zbuf.at[m, 0], zland.at[t], zl_recv).start()

                    @pl.when(b != t)
                    def _(whole=whole):
                        whole.start()
                else:
                    whole.start()

    pltpu.make_async_copy(zland, zland, zl_recv).wait()
    result = zland[0].astype(F32)
    for i in range(1, 8):
        result = result + zland[i].astype(F32)
    out_ref[...] = (result + bd_ref[...]).astype(BF16)

    swap_d.wait_send()
    for copy in gives:
        copy.wait_send()
    for k in range(CHUNKS):
        pltpu.make_async_copy(rs_land.at[k], rs_land.at[k], rs_send.at[k]).wait()
        pltpu.make_async_copy(rs_land.at[k], rs_land.at[k], ag_send.at[k]).wait()
        remote(zh_send.at[k], zh_land.at[k], zh_ss.at[k], zh_rs.at[k], opposite).wait_send()

        @pl.when(c != half)
        def _(k=k):
            remote(fown.at[k], fown.at[k], own_send.at[k], ag_recv.at[k, pair], partner).wait_send()

    for m in range(4):
        b = m + c * (7 - 2 * m)

        @pl.when(b != t)
        def _(m=m):
            remote(zbuf.at[m, 0], zland.at[t], zl_send.at[m, 0], zl_recv, partner).wait_send()

        remote(zbuf.at[m, 1], zland.at[t], zl_send.at[m, 1], zl_recv, partner).wait_send()


def per_device(residuals, w_enc, b_enc, w_dec, b_dec, act_slots):
    dma = pltpu.SemaphoreType.DMA
    return pl.pallas_call(
        kernel,
        out_shape=pltpu.VMEM((64, 256), BF16),
        in_specs=[pl.BlockSpec(memory_space=pltpu.SMEM)]
        + [pl.BlockSpec(memory_space=pl.ANY)] * 4
        + [pl.BlockSpec(memory_space=pltpu.VMEM)],
        out_specs=pl.BlockSpec(memory_space=pltpu.VMEM),
        scratch_shapes=[
            pltpu.VMEM((2, 512, 128), BF16),
            pltpu.VMEM((2, 16, 128, 128), BF16),
            pltpu.VMEM((16, 2, 128), F32),
            pltpu.VMEM((2, 2, 16, 128, 256), BF16),
            pltpu.VMEM((8, 64, 512), F32),
            pltpu.VMEM((8, 64, 512), F32),
            pltpu.VMEM((8, 64, 512), F32),
            pltpu.VMEM((8, 64, 512), BF16),
            pltpu.VMEM((CHUNKS, 15, 16, 512), BF16),
            pltpu.VMEM((CHUNKS, 16, 512), BF16),
            pltpu.VMEM((CHUNKS, 16, 512), BF16),
            pltpu.VMEM((CHUNKS, 16, 512), BF16),
            pltpu.VMEM((CHUNKS, 2, 2, 64, 512), BF16),
            pltpu.VMEM((4, 2, 64, 256), BF16),
            pltpu.VMEM((8, 64, 256), BF16),
            dma((4,)),
            dma((4, 2)),
            dma((4, 2)),
            dma,
            dma,
            dma((CHUNKS,)),
            dma((CHUNKS,)),
            pltpu.SemaphoreType.REGULAR,
            dma((CHUNKS,)),
            dma((CHUNKS,)),
            dma((CHUNKS,)),
            dma((CHUNKS,)),
            dma((CHUNKS, 2)),
            dma((4, 2)),
            dma,
        ],
        compiler_params=pltpu.CompilerParams(
            collective_id=0, has_side_effects=True, vmem_limit_bytes=60 * 2**20
        ),
        cost_estimate=pl.CostEstimate(flops=402653184, bytes_accessed=4194304, transcendentals=0),
    )(act_slots, residuals, w_enc, b_enc, w_dec.reshape(2, 16, 128, 256), b_dec.reshape(1, 256))


def solution(mesh):
    in_specs = (
        P(None, None, "layer"),
        P(None, "layer", "tok"),
        P(None, "tok"),
        P(None, "tok", "layer"),
        P("layer"),
        P(),
    )
    return jax.shard_map(
        per_device, mesh=mesh, in_specs=in_specs, out_specs=P("tok", "layer"), check_vma=False
    )
```

```python
import functools

import jax
import jax.numpy as jnp
from jax import lax
from jax.experimental import pallas as pl
from jax.experimental.pallas import tpu as pltpu
from jax.sharding import PartitionSpec as P

MESH = pl.DeviceIdType.MESH
CHUNKS = 2
F32 = jnp.float32
BF16 = jnp.bfloat16
FAR_FIRST = (10, 6, 9, 11, 14, 2, 5, 7, 8, 13, 15, 1, 3, 4, 12)


def device(x, y, zh, c, t):
    return (((x * 4 + y) * 2 + zh) * 2 + c, t)


def kernel(
    slots_ref, x_hbm, we_hbm, be_hbm, wd_hbm, bd_ref, out_ref,
    xv, we, be, wd, keep, give, take, pbuf, rs_land, zh_send, zh_land, fown, feat, zbuf, zland,
    local_sem, give_send, give_recv, wd_send, wd_recv, rs_send, rs_recv, zh_ready, line_ready, zh_ss, zh_rs,
    ag_send, own_send, ag_recv, zl_send, zl_recv,
):
    layer = lax.axis_index("layer")
    t = lax.axis_index("tok")
    c = lax.rem(layer, 2)
    zh = lax.rem(layer // 2, 2)
    y = lax.rem(layer // 4, 4)
    x = layer // 16
    half = x // 2
    pair = lax.rem(x, 2)
    crossed = lax.rem(half + c, 2)
    partner = device(x, y, zh, 1 - c, t)
    opposite = device(x, y, 1 - zh, c, t)
    across = lax.rem(t + 4, 8)
    relay = device(x, y, zh, c, across)
    u = t + c * (7 - 2 * t)

    def plane(d):
        return lax.rem(x + d // 4, 4), lax.rem(y + lax.rem(d, 4), 4)

    barrier = pltpu.get_barrier_semaphore()

    def signal(dev):
        pl.semaphore_signal(barrier, inc=1, device_id=dev, device_id_type=MESH)

    def greet_other(d, carry):
        px, py = 2 * c + d // 4, lax.rem(d, 4)

        @pl.when((px != x) | (py != y))
        def _():
            signal(device(px, py, zh, 1 - c, t))

        return carry

    def greet_line(pt, carry):
        @pl.when((pt != t) & (pt - t <= 4) & (t - pt <= 4))
        def _():
            signal(device(x, y, zh, t // 4, pt))

        return carry

    for d in FAR_FIRST:
        px, py = plane(d)
        signal(device(px, py, zh, c, t))
    lax.fori_loop(0, 8, greet_other, 0)
    signal(partner)
    lax.fori_loop(0, 8, greet_line, 0)

    @pl.when(t // 4 != c)
    def _():
        signal(relay)


    @pl.when(zh == 0)
    def _():
        signal(device(x, y, 1, c, across))

    load_x = pltpu.make_async_copy(x_hbm, xv, local_sem.at[0])
    load_d = pltpu.make_async_copy(wd_hbm, wd.at[0], local_sem.at[3])
    load_x.start()
    for s in range(2):
        for i in range(16):
            cut = pl.ds(i * 128, 128)
            pltpu.make_async_copy(we_hbm.at[s, :, cut], we.at[s, i], local_sem.at[1]).start()
    load_d.start()
    for i in range(16):
        pltpu.make_async_copy(be_hbm.at[:, pl.ds(i * 128, 128)], be.at[i], local_sem.at[2]).start()
    load_x.wait()
    pltpu.make_async_copy(we, we, local_sem.at[1]).wait()

    def remote(src, dst, send, recv, dev):
        return pltpu.make_async_remote_copy(
            src_ref=src, dst_ref=dst, send_sem=send, recv_sem=recv, device_id=dev, device_id_type=MESH
        )

    def block_id(source, b, s):
        slot = slots_ref[source, b, 4 * t + s]
        return jnp.maximum(slot - 16 * t, 0), jnp.minimum(slot + 1, 1)

    for target, source in ((keep, c), (give, 1 - c)):
        for b in range(8):
            w = jnp.concatenate([we[source, block_id(source, b, s)[0]] for s in range(4)], axis=1)
            target[b] = jnp.dot(xv[source, pl.ds(b * 64, 64), :], w, preferred_element_type=F32)

    line = (u // 4) * (16 - 2 * u) + (1 - u // 4) * 7
    pl.semaphore_wait(barrier, 15 + 15 * crossed + 1 + line + zh)

    @pl.when(zh == 1)
    def _():
        pl.semaphore_signal(
            zh_ready, inc=1, device_id=device(x, y, 0, c, across), device_id_type=MESH
        )

    pl.semaphore_signal(line_ready, inc=1, device_id=relay, device_id_type=MESH)

    gives = []
    order = []
    for m in range(4):
        for i in range(2):
            side = half if i == 0 else 1 - half
            n = m + side * (7 - 2 * m)
            order.append((m, i, side, n))
            gives.append(
                remote(give.at[n], take.at[n], give_send.at[m, i], give_recv.at[m, i], partner)
            )
            gives[-1].start()
    def send_block(m, i, side, n, copy):
        k, px = m // 2, 2 * side + m % 2
        dx = lax.rem(px - x + 4, 4)
        copy.wait_recv()
        pbuf[n] = (keep[n] + take[n]).astype(BF16)

        def send_part(j, carry, k=k, px=px, dx=dx, n=n):
            py = lax.rem(y + j, 4)
            remote(
                pbuf.at[n, pl.ds(pl.multiple_of(py * 16, 16), 16)], rs_land.at[k, 4 * dx + j - 1],
                rs_send.at[k], rs_recv.at[k], device(px, py, zh, c, t),
            ).start()
            return carry

        lax.fori_loop(1, 4, send_part, 0)
        if i == 0:

            @pl.when(px != x)
            def _(send_part=send_part):
                send_part(0, 0)
        else:
            send_part(0, 0)

    first = 4
    for o, copy in zip(order[:first], gives[:first]):
        send_block(*o, copy)

    swap_d = remote(wd_hbm, wd.at[1], wd_send, wd_recv, partner)

    @pl.when(zh == 0)
    def _():
        pl.semaphore_wait(zh_ready, 1)

    pl.semaphore_wait(line_ready, 1)

    rows = pl.ds(pl.multiple_of(y * 16, 16), 16)
    sums = []
    for k in range(CHUNKS):
        pltpu.make_async_copy(rs_land.at[k], rs_land.at[k], rs_recv.at[k]).wait()
        m = 2 * k + pair
        total = pbuf[m + half * (7 - 2 * m), rows, :].astype(F32)
        for d in range(15):
            total = total + rs_land[k, d].astype(F32)
        sums.append(total)
        zh_send[k] = total.astype(BF16)
        remote(zh_send.at[k], zh_land.at[k], zh_ss.at[k], zh_rs.at[k], opposite).start()
        if k == 0:
            for o, copy in zip(order[first:], gives[first:]):
                send_block(*o, copy)

    swap_d.start()

    pltpu.make_async_copy(be, be, local_sem.at[2]).wait()
    for k in range(CHUNKS):
        m = 2 * k + pair
        b = m + half * (7 - 2 * m)
        biases, masks = [], []
        for s in range(4):
            i, live = block_id(c, b, s)
            both = be[i]
            biases.append(jnp.where(c == 0, both[0:1], both[1:2]))
            masks.append(jnp.full((1, 128), live.astype(F32)))
        bias = jnp.concatenate(biases, axis=1)
        mask = jnp.concatenate(masks, axis=1)
        remote(zh_send.at[k], zh_land.at[k], zh_ss.at[k], zh_rs.at[k], opposite).wait_recv()
        pre = sums[k] + zh_land[k].astype(F32) + bias
        fown[k] = (jnp.maximum(pre, 0.0) * mask).astype(BF16)
        mine = feat.at[k, pair, c, rows]

        for d in FAR_FIRST:
            px, py = plane(d)
            remote(fown.at[k], mine, ag_send.at[k], ag_recv.at[k, pair], device(px, py, zh, half, t)).start()

        @pl.when(c == half)
        def _(k=k, mine=mine):
            pltpu.make_async_copy(fown.at[k], mine, ag_recv.at[k, pair]).start()

        @pl.when(c != half)
        def _(k=k, mine=mine):
            remote(fown.at[k], mine, own_send.at[k], ag_recv.at[k, pair], partner).start()

    load_d.wait()
    swap_d.wait_recv()
    for k in range(CHUNKS):
        for j in range(2):
            m = 2 * k + j
            b = m + c * (7 - 2 * m)
            pltpu.make_async_copy(feat.at[k, j], feat.at[k, j], ag_recv.at[k, j]).wait()
            ids = [[block_id(s, b, i)[0] for i in range(4)] for s in range(2)]
            f = jnp.concatenate([feat[k, j, 0], feat[k, j, 1]], axis=1)

            for side in (1, 0):
                w = jnp.concatenate([wd[side, s, ids[s][i]] for s in range(2) for i in range(4)], axis=0)
                zbuf[m, side] = jnp.dot(f, w, preferred_element_type=F32).astype(BF16)
                core = c if side == 0 else 1 - c
                whole = remote(
                    zbuf.at[m, side], zland.at[t], zl_send.at[m, side], zl_recv, device(x, y, zh, core, b)
                )
                if side == 0:

                    @pl.when(b == t)
                    def _(m=m):
                        pltpu.make_async_copy(zbuf.at[m, 0], zland.at[t], zl_recv).start()

                    @pl.when(b != t)
                    def _(whole=whole):
                        whole.start()
                else:
                    whole.start()

    pltpu.make_async_copy(zland, zland, zl_recv).wait()
    result = zland[0].astype(F32)
    for i in range(1, 8):
        result = result + zland[i].astype(F32)
    out_ref[...] = (result + bd_ref[...]).astype(BF16)

    swap_d.wait_send()
    for copy in gives:
        copy.wait_send()
    for k in range(CHUNKS):
        pltpu.make_async_copy(rs_land.at[k], rs_land.at[k], rs_send.at[k]).wait()
        pltpu.make_async_copy(rs_land.at[k], rs_land.at[k], ag_send.at[k]).wait()
        remote(zh_send.at[k], zh_land.at[k], zh_ss.at[k], zh_rs.at[k], opposite).wait_send()

        @pl.when(c != half)
        def _(k=k):
            remote(fown.at[k], fown.at[k], own_send.at[k], ag_recv.at[k, pair], partner).wait_send()

    for m in range(4):
        b = m + c * (7 - 2 * m)

        @pl.when(b != t)
        def _(m=m):
            remote(zbuf.at[m, 0], zland.at[t], zl_send.at[m, 0], zl_recv, partner).wait_send()

        remote(zbuf.at[m, 1], zland.at[t], zl_send.at[m, 1], zl_recv, partner).wait_send()


def per_device(residuals, w_enc, b_enc, w_dec, b_dec, act_slots):
    dma = pltpu.SemaphoreType.DMA
    return pl.pallas_call(
        kernel,
        out_shape=pltpu.VMEM((64, 256), BF16),
        in_specs=[pl.BlockSpec(memory_space=pltpu.SMEM)]
        + [pl.BlockSpec(memory_space=pl.ANY)] * 4
        + [pl.BlockSpec(memory_space=pltpu.VMEM)],
        out_specs=pl.BlockSpec(memory_space=pltpu.VMEM),
        scratch_shapes=[
            pltpu.VMEM((2, 512, 128), BF16),
            pltpu.VMEM((2, 16, 128, 128), BF16),
            pltpu.VMEM((16, 2, 128), F32),
            pltpu.VMEM((2, 2, 16, 128, 256), BF16),
            pltpu.VMEM((8, 64, 512), F32),
            pltpu.VMEM((8, 64, 512), F32),
            pltpu.VMEM((8, 64, 512), F32),
            pltpu.VMEM((8, 64, 512), BF16),
            pltpu.VMEM((CHUNKS, 15, 16, 512), BF16),
            pltpu.VMEM((CHUNKS, 16, 512), BF16),
            pltpu.VMEM((CHUNKS, 16, 512), BF16),
            pltpu.VMEM((CHUNKS, 16, 512), BF16),
            pltpu.VMEM((CHUNKS, 2, 2, 64, 512), BF16),
            pltpu.VMEM((4, 2, 64, 256), BF16),
            pltpu.VMEM((8, 64, 256), BF16),
            dma((4,)),
            dma((4, 2)),
            dma((4, 2)),
            dma,
            dma,
            dma((CHUNKS,)),
            dma((CHUNKS,)),
            pltpu.SemaphoreType.REGULAR,
            pltpu.SemaphoreType.REGULAR,
            dma((CHUNKS,)),
            dma((CHUNKS,)),
            dma((CHUNKS,)),
            dma((CHUNKS,)),
            dma((CHUNKS, 2)),
            dma((4, 2)),
            dma,
        ],
        compiler_params=pltpu.CompilerParams(
            collective_id=0, has_side_effects=True, vmem_limit_bytes=60 * 2**20
        ),
        cost_estimate=pl.CostEstimate(flops=402653184, bytes_accessed=4194304, transcendentals=0),
    )(act_slots, residuals, w_enc, b_enc, w_dec.reshape(2, 16, 128, 256), b_dec.reshape(1, 256))


def solution(mesh):
    in_specs = (
        P(None, None, "layer"),
        P(None, "layer", "tok"),
        P(None, "tok"),
        P(None, "tok", "layer"),
        P("layer"),
        P(),
    )
    return jax.shard_map(
        per_device, mesh=mesh, in_specs=in_specs, out_specs=P("tok", "layer"), check_vma=False
    )
```
